32 devices in a mesh: ctx: 8 (over z, x), chan: 4 (over y, core).
Axes of the slice: x: 2, y: 2, z: 4, core: 2. Of those that a mesh axis runs over, the one named last changes fastest.
Arguments:
- signal: bfloat16 [2048, 4096], P('ctx', 'chan'), may hold values from -6 to 6
- gate_values: bfloat16 [2048, 4096], P('ctx', 'chan'), may hold values from -6 to 6
- skip_gain: float32 [4096], P('chan'), may hold values from 0.5 to 1.5
- filter_base: bfloat16 [64, 16384], P('chan', 'ctx'), may hold values from -0.09375 to 0.09375
- decay_rate: float32 [64], P('chan'), may hold values from 0.3 to 30
- filter_depth: int32 [64], P('chan'), may hold values from 2048 to 16384
- doc_starts: int32 [5], replicated, may hold values from 0 to 512, as said below
Outputs:
- mixed: bfloat16 [2048, 4096], P('ctx', 'chan')
The draws below stay inside these ranges and needn't reach their ends.
Inputs may be any that keep to these rules, and one draw needn't show every extreme that they name: doc_starts[0] is 0 and the starts rise strictly; document k runs from doc_starts[k] up to the position before the next start, the last one to the end of the window.
All inputs are finite; a program needn't handle non-finite values.
Results may differ from the reference program's by a relative error of at most 0.0026.
Values may be sent and summed in bfloat16 or wider, within the bound.
A program may use at most 64 MiB of HBM per device.

```python
import math
import jax
import jax.numpy as jnp
from jax import lax

CHANNELS = 4096
LAGS = 16384
GROUP = 64
DOCS = 5
SEQ = 2048
GROUPS = 64


def draw_filter_depth(key, part):
    first_key, second_key, third_key = jax.random.split(key, 3)
    depths = jax.random.randint(first_key, (GROUPS,), LAGS // 8, LAGS + 1)
    high_group = jax.random.randint(second_key, (), 0, GROUPS)
    low_group = (high_group + 1 + jax.random.randint(third_key, (), 0, GROUPS - 1)) % GROUPS
    indices = jnp.arange(GROUPS)
    depths = jnp.where(indices == high_group, LAGS, depths)
    depths = jnp.where(indices == low_group, LAGS // 8, depths)
    return depths.astype(jnp.int32)


def draw_doc_starts(key, part):
    shuffled = jax.random.permutation(key, SEQ // 4 - 1)[:DOCS - 2] + 1
    interior = jnp.sort(shuffled).astype(jnp.int32)
    return jnp.concatenate([jnp.zeros((1,), jnp.int32), interior, jnp.full((1,), SEQ // 4, jnp.int32)])


def shard_levels(rng, dims, cuts, least, top_value):
    gain, own = 1.0, jax.random.fold_in(rng, 6)
    for dim, blocks in cuts:
        steps = jnp.exp(jax.random.uniform(jax.random.fold_in(own, dim), (blocks,), jnp.float32, least / len(cuts), top_value / len(cuts)))
        gain = gain * jnp.repeat(steps, dims[dim] // blocks).reshape([-1 if axis == dim else 1 for axis in range(len(dims))])
    return gain


def normal_values(own_key, shape, deviation, limit, pieces=(), kind=jnp.bfloat16):
    entries = deviation * jax.random.normal(own_key, shape, jnp.float32)
    if pieces:
        entries = entries * shard_levels(own_key, shape, pieces, -0.22, 0.18)
    return jnp.clip(entries, -limit, limit).astype(kind)


def setup_inputs(seed: int = 0) -> dict:
    streams_of = jax.random.split(jax.random.key(seed), 8)
    return {
        "signal": normal_values(streams_of[0], (SEQ, CHANNELS), 1.0, 6.0, ((0, 8), (1, 4))),
        "gate_values": normal_values(streams_of[1], (SEQ, CHANNELS), 1.0, 6.0, ((0, 8), (1, 4))),
        "skip_gain": jnp.clip(0.5 + 1.0 * jax.random.uniform(streams_of[2], (CHANNELS,), jnp.float32) ** shard_levels(streams_of[2], (CHANNELS,), ((0, 4),), -0.2, 0.2), 0.5, 1.5),
        "filter_base": normal_values(streams_of[3], (GROUPS, LAGS), (LAGS // 4) ** -0.5, 0.09375, ((0, 4), (1, 8))),
        "decay_rate": jnp.clip(jnp.exp(math.log(30.0) - 4.6051701 * jax.random.uniform(streams_of[4], (GROUPS,), jnp.float32) ** shard_levels(streams_of[4], (GROUPS,), ((0, 4),), -0.2, 0.2)), 0.3, 30.0),
        "filter_depth": draw_filter_depth(jax.random.fold_in(streams_of[7], 71), 0),
        "doc_starts": draw_doc_starts(jax.random.fold_in(streams_of[7], 71), 0),
    }


def reference(signal, gate_values, skip_gain, filter_base, decay_rate, filter_depth, doc_starts):
    lag_index = jnp.arange(LAGS, dtype=jnp.int32)
    lag_float = lag_index.astype(jnp.float32)
    inside = lag_index[None, :] < filter_depth[:, None]
    filters = jnp.where(inside, filter_base.astype(jnp.float32) * jnp.exp(-decay_rate[:, None] * lag_float[None, :] / LAGS), 0.0).astype(jnp.bfloat16)
    per_channel = jnp.repeat(filters.astype(jnp.float32), GROUP, axis=0)
    values = signal.astype(jnp.float32)
    positions = jnp.arange(SEQ, dtype=jnp.int32)
    doc_index = jnp.sum((positions[:, None] >= doc_starts[None, :]).astype(jnp.int32), axis=1) - 1
    transform_size = 1 << (SEQ + LAGS - 1).bit_length()
    block_width = math.gcd(CHANNELS, 512)
    block_count = CHANNELS // block_width

    def one_block(operands):
        filter_taps, inputs = operands
        spectrum = jnp.fft.rfft(filter_taps, n=transform_size, axis=1).T
        summed = jnp.zeros_like(inputs)
        for k in range(DOCS):
            member = (doc_index == k)[:, None]
            spectra = jnp.fft.rfft(jnp.where(member, inputs, 0.0), n=transform_size, axis=0)
            result = jnp.fft.irfft(spectra * spectrum, n=transform_size, axis=0)[:SEQ]
            summed = summed + jnp.where(member, result, 0.0)
        return summed

    taps_blocks = per_channel.reshape(block_count, block_width, LAGS)
    input_blocks = values.reshape(SEQ, block_count, block_width).transpose(1, 0, 2)
    convolved = lax.map(one_block, (taps_blocks, input_blocks))
    convolved = convolved.transpose(1, 0, 2).reshape(SEQ, CHANNELS)
    mixed = gate_values.astype(jnp.float32) * (convolved + skip_gain[None, :] * values)
    return mixed.astype(jnp.bfloat16)
```

```python
import functools

import jax
import jax.numpy as jnp
from jax import lax
from jax.experimental import pallas as pl
from jax.experimental.pallas import tpu as pltpu
from jax.sharding import PartitionSpec as P

LAGS = 16384


def begin_rows(doc_starts, positions):
    return jnp.max(
        jnp.where(doc_starts[None, :] <= positions[:, None], doc_starts[None, :], 0), axis=1
    )


def toeplitz_apply(summed, padded, margin, lag_total, out_first, doc_begin, source, anchor):
    out_rows, chan_width = summed.shape
    group_count = padded.shape[0]
    group_size = chan_width // group_count
    source_rows = source.shape[0]
    window_size = out_rows + source_rows - 1
    lowest = out_first - anchor - source_rows + 1
    offset = jnp.clip(lowest, -window_size, lag_total) + margin
    window = lax.dynamic_slice_in_dim(padded, offset, window_size, 1)
    extended = jnp.pad(window, ((0, 0), (0, 1)))
    repeated = jnp.tile(extended, (1, out_rows + 1))
    skewed = repeated[:, : out_rows * (window_size + 2)].reshape(
        group_count, out_rows, window_size + 2
    )
    toeplitz = skewed[:, :, :source_rows][:, :, ::-1]
    doc_mask = (anchor + lax.iota(jnp.int32, source_rows))[None, :] >= doc_begin[:, None]
    toeplitz = jnp.where(doc_mask[None], toeplitz, jnp.zeros((), jnp.bfloat16))
    channels = source.reshape(source_rows, group_count, group_size)
    product = jnp.einsum("gts,sgc->tgc", toeplitz, channels, preferred_element_type=jnp.float32)
    return summed + product.reshape(out_rows, chan_width)


def gathered_body(signal, gate_values, skip_gain, filter_base, decay_rate, filter_depth, doc_starts):
    tok_rows, chan_width = signal.shape
    group_count, lag_width = filter_base.shape
    ctx_index = lax.axis_index("ctx")
    lag_index = ctx_index * lag_width + lax.iota(jnp.int32, lag_width)
    inside = lag_index[None, :] < filter_depth[:, None]
    local_panel = jnp.where(
        inside,
        filter_base.astype(jnp.float32)
        * jnp.exp(-decay_rate[:, None] * lag_index.astype(jnp.float32)[None, :] / LAGS),
        0.0,
    ).astype(jnp.bfloat16)
    filters = lax.all_gather(local_panel, "ctx", axis=1, tiled=True)
    lag_total = filters.shape[1]
    margin = 2 * tok_rows
    padded = jnp.pad(filters, ((0, 0), (margin, margin)))
    first_row = ctx_index * tok_rows
    positions = first_row + lax.iota(jnp.int32, tok_rows)
    doc_begin = begin_rows(doc_starts, positions)

    def add_checked(summed, source, anchor):
        needed = anchor < first_row + tok_rows
        return lax.cond(
            needed,
            lambda carried: toeplitz_apply(
                carried, padded, margin, lag_total, first_row, doc_begin, source, anchor
            ),
            lambda carried: carried,
            summed,
        )

    initial = jnp.zeros((tok_rows, chan_width), jnp.float32)
    summed = initial
    source = lax.all_gather(signal, "ctx", axis=0, tiled=True)
    source_rows = source.shape[0]
    steps_count = source_rows // tok_rows
    stacked = source.reshape(steps_count, tok_rows, chan_width)

    def advance(carried, item):
        one_shard, number = item
        return (add_checked(carried, one_shard, number * tok_rows), None)

    summed, ignored = lax.scan(advance, summed, (stacked, jnp.arange(steps_count, dtype=jnp.int32)))
    mixed = gate_values.astype(jnp.float32) * (
        summed + skip_gain[None, :] * signal.astype(jnp.float32)
    )
    return mixed.astype(jnp.bfloat16)


LINK = jnp.int16
TOP = 32000.0
TAIL = 16
MESH = pl.DeviceIdType.MESH


def store_coded(y_buf, block, total):
    rows, width = total.shape
    peak = jnp.maximum(jnp.max(jnp.abs(total), axis=0, keepdims=True), 1e-30)
    exponent = jnp.ceil(jnp.log2(peak))
    coded = jnp.floor(total * (jnp.exp2(-exponent) * TOP) + 0.5)
    first = block * (rows + TAIL)
    y_buf[pl.ds(first, rows), :] = coded.astype(jnp.int32).astype(LINK)
    tail = jnp.broadcast_to(exponent, (TAIL, width))
    y_buf[pl.ds(first + rows, TAIL), :] = tail.astype(jnp.int32).astype(LINK)


def exchange_kernel(
    count, masked_blocks, signal_ref, taps_ref, starts_ref, out_ref,
    taps_buf, x_buf, y_buf, strip, local_sems, taps_send, taps_recv, send_x, recv_x, send_y, recv_y,
):
    me = lax.axis_index("ctx")
    rows = x_buf.shape[0] // count
    width = x_buf.shape[1]
    tap_rows = taps_buf.shape[0]
    groups = tap_rows // count
    window = rows * count

    def peer_at(offset):
        return lax.rem(me + offset, count)

    def lanes(index):
        return pl.ds(pl.multiple_of(index * width, width), width)

    def row_block(index):
        return pl.ds(pl.multiple_of(index * rows, rows), rows)

    def coded_block(index):
        return pl.ds(pl.multiple_of(index * (rows + TAIL), rows + TAIL), rows + TAIL)

    own_x = pltpu.make_async_copy(
        signal_ref.at[:, lanes(me)], x_buf.at[row_block(me)], local_sems.at[0]
    )
    own_x.start()

    barrier = pltpu.get_barrier_semaphore()
    for offset in range(1, count):
        pl.semaphore_signal(
            barrier, inc=1, device_id={"ctx": peer_at(offset)}, device_id_type=MESH
        )
    pl.semaphore_wait(barrier, count - 1)

    def taps_copy(peer):
        return pltpu.make_async_remote_copy(
            src_ref=taps_ref.at[pl.ds(peer * tap_rows, tap_rows)],
            dst_ref=taps_buf,
            send_sem=taps_send.at[peer],
            recv_sem=taps_recv,
            device_id={"ctx": jnp.int32(peer)},
            device_id_type=MESH,
        )

    @pl.when(me == 0)
    def _():
        for peer in range(1, count):
            taps_copy(peer).start()
        own = pltpu.make_async_copy(taps_ref.at[pl.ds(0, tap_rows)], taps_buf, local_sems.at[1])
        own.start()
        own.wait()

    def x_copy(offset):
        return pltpu.make_async_remote_copy(
            src_ref=signal_ref.at[:, lanes(peer_at(offset))],
            dst_ref=x_buf.at[row_block(me)],
            send_sem=send_x.at[offset],
            recv_sem=recv_x.at[offset],
            device_id={"ctx": peer_at(offset)},
            device_id_type=MESH,
        )

    def x_arrival(offset):
        return pltpu.make_async_remote_copy(
            src_ref=signal_ref.at[:, lanes(peer_at(offset))],
            dst_ref=x_buf.at[row_block(peer_at(count - offset))],
            send_sem=send_x.at[offset],
            recv_sem=recv_x.at[offset],
            device_id={"ctx": peer_at(offset)},
            device_id_type=MESH,
        )

    for offset in range(1, count):
        x_copy(offset).start()

    @pl.when(me != 0)
    def _():
        taps_copy(1).wait_recv()

    row_id = lax.broadcasted_iota(jnp.int32, (rows, rows), 0)
    col_id = lax.broadcasted_iota(jnp.int32, (rows, rows), 1)
    flip = (row_id + col_id == rows - 1).astype(jnp.bfloat16)
    flipped = jnp.dot(taps_buf[...], flip, preferred_element_type=jnp.float32)
    span = window + rows
    step = 32
    for g in range(groups):
        pieces = [
            flipped[g * count + d : g * count + d + 1, :] for d in range(count - 1, -1, -1)
        ]
        line = jnp.concatenate(pieces + [jnp.zeros((1, rows), jnp.float32)], axis=1)
        spread = jnp.broadcast_to(line, (step, span))
        for base in range(0, rows, step):
            turned = pltpu.roll(
                spread, (span - (rows - 1) + base) % span, 1, stride=1, stride_axis=0
            )
            strip[g, pl.ds(base, step), :] = turned[:, :window].astype(jnp.bfloat16)

    own_x.wait()
    for offset in range(1, count):
        x_arrival(offset).wait_recv()

    docs = starts_ref.shape[0]
    last_start = starts_ref[docs - 1]
    head_rows = masked_blocks * rows
    x_head = x_buf[pl.ds(0, head_rows), :]
    head_id = lax.broadcasted_iota(jnp.int32, (head_rows, width), 0)
    x_head_masked = jnp.where(
        head_id >= last_start, x_head.astype(jnp.float32), 0.0
    ).astype(jnp.bfloat16)
    lane_group = lax.broadcasted_iota(jnp.int32, (rows, width), 1) // (width // groups)

    for block in range(masked_blocks):
        depth = (block + 1) * rows
        t_id = block * rows + lax.broadcasted_iota(jnp.int32, (rows, depth), 0)
        s_id = lax.broadcasted_iota(jnp.int32, (rows, depth), 1)
        begin = jnp.zeros((rows, depth), jnp.int32)
        for k in range(docs):
            begin = jnp.where(starts_ref[k] <= t_id, jnp.maximum(begin, starts_ref[k]), begin)
        seen = s_id >= begin
        total = jnp.zeros((rows, width), jnp.float32)
        for g in range(groups):
            taps = jnp.where(
                seen, strip[g, :, pl.ds(window - depth, depth)].astype(jnp.float32), 0.0
            ).astype(jnp.bfloat16)
            part = jnp.dot(taps, x_head[:depth], preferred_element_type=jnp.float32)
            total = jnp.where(lane_group == g, part, total)
        store_coded(y_buf, block, total)

    x_buf[pl.ds(0, head_rows), :] = x_head_masked
    for block in range(masked_blocks, count):
        depth = (block + 1) * rows
        total = jnp.zeros((rows, width), jnp.float32)
        for g in range(groups):
            part = jnp.dot(
                strip[g, :, pl.ds(window - depth, depth)],
                x_buf[pl.ds(0, depth), :],
                preferred_element_type=jnp.float32,
            )
            total = jnp.where(lane_group == g, part, total)
        store_coded(y_buf, block, total)

    own_y = pltpu.make_async_copy(
        y_buf.at[coded_block(me)], out_ref.at[:, lanes(me)], local_sems.at[2]
    )
    own_y.start()

    def y_copy(offset):
        return pltpu.make_async_remote_copy(
            src_ref=y_buf.at[coded_block(peer_at(offset))],
            dst_ref=out_ref.at[:, lanes(me)],
            send_sem=send_y.at[offset],
            recv_sem=recv_y.at[offset],
            device_id={"ctx": peer_at(offset)},
            device_id_type=MESH,
        )

    def y_arrival(offset):
        return pltpu.make_async_remote_copy(
            src_ref=y_buf.at[coded_block(peer_at(offset))],
            dst_ref=out_ref.at[:, lanes(peer_at(count - offset))],
            send_sem=send_y.at[offset],
            recv_sem=recv_y.at[offset],
            device_id={"ctx": peer_at(offset)},
            device_id_type=MESH,
        )

    for offset in range(1, count):
        y_copy(offset).start()

    @pl.when(me == 0)
    def _():
        for peer in range(1, count):
            taps_copy(peer).wait_send()

    for offset in range(1, count):
        x_copy(offset).wait_send()
    own_y.wait()
    for offset in range(1, count):
        y_arrival(offset).wait_recv()
    for offset in range(1, count):
        y_copy(offset).wait_send()


def exchanged_body(
    count, signal, gate_values, skip_gain, filter_base, decay_rate, filter_depth, doc_starts
):
    tok_rows, chan_width = signal.shape
    group_count, lag_width = filter_base.shape
    window = tok_rows * count
    ctx_index = lax.axis_index("ctx")
    lag_index = ctx_index * lag_width + lax.iota(jnp.int32, window)
    inside = lag_index[None, :] < filter_depth[:, None]
    panel = jnp.where(
        inside,
        filter_base[:, :window].astype(jnp.float32)
        * jnp.exp(-decay_rate[:, None] * lag_index.astype(jnp.float32)[None, :] / LAGS),
        0.0,
    ).astype(jnp.bfloat16)
    taps = panel.reshape(group_count * count, tok_rows)
    width = chan_width // count
    tap_rows = group_count
    groups = group_count // count
    masked_blocks = max(1, count // 4)
    convolved = pl.pallas_call(
        functools.partial(exchange_kernel, count, masked_blocks),
        out_shape=jax.ShapeDtypeStruct((tok_rows + TAIL, chan_width), LINK),
        in_specs=[
            pl.BlockSpec(memory_space=pl.ANY),
            pl.BlockSpec(memory_space=pl.ANY),
            pl.BlockSpec(memory_space=pltpu.SMEM),
        ],
        out_specs=pl.BlockSpec(memory_space=pl.ANY),
        scratch_shapes=[
            pltpu.VMEM((tap_rows, tok_rows), jnp.bfloat16),
            pltpu.VMEM((window, width), jnp.bfloat16),
            pltpu.VMEM((window + count * TAIL, width), LINK),
            pltpu.VMEM((groups, tok_rows, window), jnp.bfloat16),
            pltpu.SemaphoreType.DMA((3,)),
            pltpu.SemaphoreType.DMA((count,)),
            pltpu.SemaphoreType.DMA,
            pltpu.SemaphoreType.DMA((count,)),
            pltpu.SemaphoreType.DMA((count,)),
            pltpu.SemaphoreType.DMA((count,)),
            pltpu.SemaphoreType.DMA((count,)),
        ],
        compiler_params=pltpu.CompilerParams(
            collective_id=0, has_side_effects=True, vmem_limit_bytes=32 * 1024 * 1024
        ),
    )(signal, taps, doc_starts)
    unit = jnp.exp2(convolved[tok_rows : tok_rows + 1].astype(jnp.float32)) * (1.0 / TOP)
    mixed = gate_values.astype(jnp.float32) * (
        convolved[:tok_rows].astype(jnp.float32) * unit
        + skip_gain[None, :] * signal.astype(jnp.float32)
    )
    return mixed.astype(jnp.bfloat16)


def body(signal, gate_values, skip_gain, filter_base, decay_rate, filter_depth, doc_starts, count):
    tok_rows, chan_width = signal.shape
    group_count, lag_width = filter_base.shape
    whole_groups = group_count % count == 0 and chan_width % (count * 128) == 0
    fits = tok_rows == 256 and lag_width >= tok_rows * count and count % 4 == 0
    aligned = group_count % 16 == 0
    arrays = (signal, gate_values, skip_gain, filter_base, decay_rate, filter_depth, doc_starts)
    if whole_groups and fits and aligned:
        return exchanged_body(count, *arrays)
    return gathered_body(*arrays)


def solution(mesh):
    in_specs = (
        P("ctx", "chan"),
        P("ctx", "chan"),
        P("chan"),
        P("chan", "ctx"),
        P("chan"),
        P("chan"),
        P(),
    )
    out_specs = P("ctx", "chan")
    return jax.shard_map(
        functools.partial(body, count=mesh.shape["ctx"]),
        mesh=mesh,
        in_specs=in_specs,
        out_specs=out_specs,
        check_vma=False,
    )
```

```python
import functools

import jax
import jax.numpy as jnp
from jax import lax
from jax.experimental import pallas as pl
from jax.experimental.pallas import tpu as pltpu
from jax.sharding import PartitionSpec as P

LAGS = 16384


def begin_rows(doc_starts, positions):
    return jnp.max(
        jnp.where(doc_starts[None, :] <= positions[:, None], doc_starts[None, :], 0), axis=1
    )


def toeplitz_apply(summed, padded, margin, lag_total, out_first, doc_begin, source, anchor):
    out_rows, chan_width = summed.shape
    group_count = padded.shape[0]
    group_size = chan_width // group_count
    source_rows = source.shape[0]
    window_size = out_rows + source_rows - 1
    lowest = out_first - anchor - source_rows + 1
    offset = jnp.clip(lowest, -window_size, lag_total) + margin
    window = lax.dynamic_slice_in_dim(padded, offset, window_size, 1)
    extended = jnp.pad(window, ((0, 0), (0, 1)))
    repeated = jnp.tile(extended, (1, out_rows + 1))
    skewed = repeated[:, : out_rows * (window_size + 2)].reshape(
        group_count, out_rows, window_size + 2
    )
    toeplitz = skewed[:, :, :source_rows][:, :, ::-1]
    doc_mask = (anchor + lax.iota(jnp.int32, source_rows))[None, :] >= doc_begin[:, None]
    toeplitz = jnp.where(doc_mask[None], toeplitz, jnp.zeros((), jnp.bfloat16))
    channels = source.reshape(source_rows, group_count, group_size)
    product = jnp.einsum("gts,sgc->tgc", toeplitz, channels, preferred_element_type=jnp.float32)
    return summed + product.reshape(out_rows, chan_width)


def gathered_body(signal, gate_values, skip_gain, filter_base, decay_rate, filter_depth, doc_starts):
    tok_rows, chan_width = signal.shape
    group_count, lag_width = filter_base.shape
    ctx_index = lax.axis_index("ctx")
    lag_index = ctx_index * lag_width + lax.iota(jnp.int32, lag_width)
    inside = lag_index[None, :] < filter_depth[:, None]
    local_panel = jnp.where(
        inside,
        filter_base.astype(jnp.float32)
        * jnp.exp(-decay_rate[:, None] * lag_index.astype(jnp.float32)[None, :] / LAGS),
        0.0,
    ).astype(jnp.bfloat16)
    filters = lax.all_gather(local_panel, "ctx", axis=1, tiled=True)
    lag_total = filters.shape[1]
    margin = 2 * tok_rows
    padded = jnp.pad(filters, ((0, 0), (margin, margin)))
    first_row = ctx_index * tok_rows
    positions = first_row + lax.iota(jnp.int32, tok_rows)
    doc_begin = begin_rows(doc_starts, positions)

    def add_checked(summed, source, anchor):
        needed = anchor < first_row + tok_rows
        return lax.cond(
            needed,
            lambda carried: toeplitz_apply(
                carried, padded, margin, lag_total, first_row, doc_begin, source, anchor
            ),
            lambda carried: carried,
            summed,
        )

    initial = jnp.zeros((tok_rows, chan_width), jnp.float32)
    summed = initial
    source = lax.all_gather(signal, "ctx", axis=0, tiled=True)
    source_rows = source.shape[0]
    steps_count = source_rows // tok_rows
    stacked = source.reshape(steps_count, tok_rows, chan_width)

    def advance(carried, item):
        one_shard, number = item
        return (add_checked(carried, one_shard, number * tok_rows), None)

    summed, ignored = lax.scan(advance, summed, (stacked, jnp.arange(steps_count, dtype=jnp.int32)))
    mixed = gate_values.astype(jnp.float32) * (
        summed + skip_gain[None, :] * signal.astype(jnp.float32)
    )
    return mixed.astype(jnp.bfloat16)


LINK = jnp.int16
TOP = 32000.0
TAIL = 16
VMEM_BYTES = 60 * 1024 * 1024
MESH = pl.DeviceIdType.MESH


def store_coded(y_buf, block, total):
    rows, width = total.shape
    peak = jnp.maximum(jnp.max(jnp.abs(total), axis=0, keepdims=True), 1e-30)
    exponent = jnp.ceil(jnp.log2(peak))
    coded = jnp.floor(total * (jnp.exp2(-exponent) * TOP) + 0.5)
    first = block * (rows + TAIL)
    y_buf[pl.ds(first, rows), :] = coded.astype(jnp.int32).astype(LINK)
    tail = jnp.broadcast_to(exponent, (TAIL, width))
    y_buf[pl.ds(first + rows, TAIL), :] = tail.astype(jnp.int32).astype(LINK)


def exchange_kernel(
    count, masked_blocks, signal_ref, base_ref, decay_ref, depth_ref, starts_ref, out_ref,
    base_buf, taps_all, taps_buf, x_buf, y_buf, strip, decay_mem, depth_mem, starts_mem,
    local_sems, taps_send, taps_recv, send_x, recv_x, send_y, recv_y,
):
    me = lax.axis_index("ctx")
    half = count // 2
    rows = x_buf.shape[0] // count
    width = x_buf.shape[1]
    tap_rows = taps_buf.shape[0]
    groups = tap_rows // count
    window = rows * count

    def lanes(index):
        return pl.ds(pl.multiple_of(index * width, width), width)

    def row_block(index):
        return pl.ds(pl.multiple_of(index * rows, rows), rows)

    def coded_block(index):
        return pl.ds(pl.multiple_of(index * (rows + TAIL), rows + TAIL), rows + TAIL)

    barrier = pltpu.get_barrier_semaphore()
    for offset in range(1, count):
        pl.semaphore_signal(
            barrier, inc=1, device_id={"ctx": lax.rem(me + offset, count)}, device_id_type=MESH
        )

    own_x = pltpu.make_async_copy(
        signal_ref.at[:, lanes(me)], x_buf.at[row_block(me)], local_sems.at[0]
    )
    own_x.start()
    starts_copy = pltpu.make_async_copy(starts_ref, starts_mem, local_sems.at[1])
    starts_copy.start()
    base_copy = pltpu.make_async_copy(base_ref.at[:, pl.ds(0, window)], base_buf, local_sems.at[2])
    decay_copy = pltpu.make_async_copy(decay_ref, decay_mem, local_sems.at[3])
    depth_copy = pltpu.make_async_copy(depth_ref, depth_mem, local_sems.at[4])

    @pl.when(me == 0)
    def _():
        base_copy.start()
        decay_copy.start()
        depth_copy.start()

    pl.semaphore_wait(barrier, count - 1)

    def x_copy(peer):
        return pltpu.make_async_remote_copy(
            src_ref=signal_ref.at[:, lanes(peer)],
            dst_ref=x_buf.at[row_block(me)],
            send_sem=send_x.at[peer],
            recv_sem=recv_x.at[me],
            device_id={"ctx": peer},
            device_id_type=MESH,
        )

    def x_arrival(source):
        return pltpu.make_async_remote_copy(
            src_ref=signal_ref.at[:, lanes(source)],
            dst_ref=x_buf.at[row_block(source)],
            send_sem=send_x.at[source],
            recv_sem=recv_x.at[source],
            device_id={"ctx": jnp.int32(source)},
            device_id_type=MESH,
        )

    side = lax.div(me, half)
    place = lax.rem(me, half)
    near = [side * half + lax.rem(place + k, half) for k in range(1, half)]
    far = [(1 - side) * half + lax.rem(place + k, half) for k in range(half)]
    early = place < half // 2

    @pl.when(early)
    def _():
        for peer in far + near:
            x_copy(peer).start()

    @pl.when(jnp.logical_not(early))
    def _():
        for peer in near + far:
            x_copy(peer).start()

    def taps_copy(peer):
        return pltpu.make_async_remote_copy(
            src_ref=taps_all.at[pl.ds(peer * tap_rows, tap_rows)],
            dst_ref=taps_buf,
            send_sem=taps_send.at[peer],
            recv_sem=taps_recv,
            device_id={"ctx": jnp.int32(peer)},
            device_id_type=MESH,
        )

    @pl.when(me == 0)
    def _():
        base_copy.wait()
        decay_copy.wait()
        depth_copy.wait()
        group_rows = groups * count
        group_id = lax.broadcasted_iota(jnp.int32, (group_rows, 128), 0)
        decay = jnp.zeros((group_rows, 128), jnp.float32)
        depth = jnp.zeros((group_rows, 128), jnp.int32)
        for g in range(group_rows):
            decay = jnp.where(group_id == g, decay_mem[g], decay)
            depth = jnp.where(group_id == g, depth_mem[g], depth)
        decay = jnp.concatenate([decay] * (rows // 128), axis=1)
        depth = jnp.concatenate([depth] * (rows // 128), axis=1)
        out_row = lax.broadcasted_iota(jnp.int32, (group_rows * count, group_rows), 0)
        in_row = lax.broadcasted_iota(jnp.int32, (group_rows * count, group_rows), 1)
        placed = jnp.zeros((group_rows * count, rows), jnp.float32)
        for d in range(count):
            lag = d * rows + lax.broadcasted_iota(jnp.int32, (group_rows, rows), 1)
            base = base_buf[:, pl.ds(d * rows, rows)].astype(jnp.float32)
            kept = base * jnp.exp(-decay * lag.astype(jnp.float32) / LAGS)
            panel = jnp.where(lag < depth, kept, 0.0).astype(jnp.bfloat16)
            pick = (out_row == in_row * count + d).astype(jnp.float32).astype(jnp.bfloat16)
            placed += jnp.dot(pick, panel, preferred_element_type=jnp.float32)
        taps_all[...] = placed.astype(jnp.bfloat16)
        for peer in range(1, count):
            taps_copy(peer).start()
        taps_buf[...] = taps_all[pl.ds(0, tap_rows), :]

    @pl.when(me != 0)
    def _():
        taps_copy(1).wait_recv()

    row_id = lax.broadcasted_iota(jnp.int32, (rows, rows), 0)
    col_id = lax.broadcasted_iota(jnp.int32, (rows, rows), 1)
    flip = (row_id + col_id == rows - 1).astype(jnp.float32).astype(jnp.bfloat16)
    flipped = jnp.dot(taps_buf[...], flip, preferred_element_type=jnp.float32)
    span = window + rows
    step = 32
    for g in range(groups):
        pieces = [
            flipped[g * count + d : g * count + d + 1, :] for d in range(count - 1, -1, -1)
        ]
        line = jnp.concatenate(pieces + [jnp.zeros((1, rows), jnp.float32)], axis=1)
        spread = jnp.broadcast_to(line, (step, span))
        for base in range(0, rows, step):
            turned = pltpu.roll(
                spread, (span - (rows - 1) + base) % span, 1, stride=1, stride_axis=0
            )
            strip[g, pl.ds(base, step), :] = turned[:, :window].astype(jnp.bfloat16)

    starts_copy.wait()
    own_x.wait()
    docs = starts_mem.shape[0]
    head_rows = masked_blocks * rows
    lane_group = lax.broadcasted_iota(jnp.int32, (rows, width), 1) // (width // groups)

    def wait_for(block):
        @pl.when(me != block)
        def _():
            x_arrival(block).wait_recv()

    def y_copy(block):
        return pltpu.make_async_remote_copy(
            src_ref=y_buf.at[coded_block(block)],
            dst_ref=out_ref.at[:, lanes(me)],
            send_sem=send_y.at[block],
            recv_sem=recv_y.at[me],
            device_id={"ctx": jnp.int32(block)},
            device_id_type=MESH,
        )

    def y_arrival(source):
        return pltpu.make_async_remote_copy(
            src_ref=y_buf.at[coded_block(source)],
            dst_ref=out_ref.at[:, lanes(source)],
            send_sem=send_y.at[source],
            recv_sem=recv_y.at[source],
            device_id={"ctx": jnp.int32(source)},
            device_id_type=MESH,
        )

    own_y = pltpu.make_async_copy(
        y_buf.at[coded_block(me)], out_ref.at[:, lanes(me)], local_sems.at[5]
    )

    def send_back(block, total):
        store_coded(y_buf, block, total)

        @pl.when(me != block)
        def _():
            y_copy(block).start()

        @pl.when(me == block)
        def _():
            own_y.start()

    for block in range(masked_blocks):
        wait_for(block)
        depth = (block + 1) * rows
        t_id = block * rows + lax.broadcasted_iota(jnp.int32, (rows, depth), 0)
        s_id = lax.broadcasted_iota(jnp.int32, (rows, depth), 1)
        begin = jnp.zeros((rows, depth), jnp.int32)
        for k in range(docs):
            start = starts_mem[k]
            begin = jnp.where(start <= t_id, jnp.maximum(begin, start), begin)
        seen = s_id >= begin
        total = jnp.zeros((rows, width), jnp.float32)
        for g in range(groups):
            taps = jnp.where(
                seen, strip[g, :, pl.ds(window - depth, depth)].astype(jnp.float32), 0.0
            ).astype(jnp.bfloat16)
            part = jnp.dot(taps, x_buf[pl.ds(0, depth), :], preferred_element_type=jnp.float32)
            total = jnp.where(lane_group == g, part, total)
        send_back(block, total)

    head_id = lax.broadcasted_iota(jnp.int32, (head_rows, width), 0)
    x_head = x_buf[pl.ds(0, head_rows), :].astype(jnp.float32)
    x_buf[pl.ds(0, head_rows), :] = jnp.where(
        head_id >= starts_mem[docs - 1], x_head, 0.0
    ).astype(jnp.bfloat16)
    for block in range(masked_blocks, count):
        wait_for(block)
        depth = (block + 1) * rows
        total = jnp.zeros((rows, width), jnp.float32)
        for g in range(groups):
            part = jnp.dot(
                strip[g, :, pl.ds(window - depth, depth)],
                x_buf[pl.ds(0, depth), :],
                preferred_element_type=jnp.float32,
            )
            total = jnp.where(lane_group == g, part, total)
        send_back(block, total)

    @pl.when(me == 0)
    def _():
        for peer in range(1, count):
            taps_copy(peer).wait_send()

    for peer in near + far:
        x_copy(peer).wait_send()
    own_y.wait()
    for peer in near + far:
        y_arrival(peer).wait_recv()
    for peer in near + far:
        y_arrival(peer).wait_send()


def exchanged_body(
    count, signal, gate_values, skip_gain, filter_base, decay_rate, filter_depth, doc_starts
):
    tok_rows, chan_width = signal.shape
    group_count, lag_width = filter_base.shape
    window = tok_rows * count
    width = chan_width // count
    tap_rows = group_count
    groups = group_count // count
    masked_blocks = max(1, count // 4)
    convolved = pl.pallas_call(
        functools.partial(exchange_kernel, count, masked_blocks),
        out_shape=jax.ShapeDtypeStruct((tok_rows + TAIL, chan_width), LINK),
        in_specs=[
            pl.BlockSpec(memory_space=pl.ANY),
        ]
        * 5,
        out_specs=pl.BlockSpec(memory_space=pl.ANY),
        scratch_shapes=[
            pltpu.VMEM((group_count, window), jnp.bfloat16),
            pltpu.VMEM((tap_rows * count, tok_rows), jnp.bfloat16),
            pltpu.VMEM((tap_rows, tok_rows), jnp.bfloat16),
            pltpu.VMEM((window, width), jnp.bfloat16),
            pltpu.VMEM((window + count * TAIL, width), LINK),
            pltpu.VMEM((groups, tok_rows, window), jnp.bfloat16),
            pltpu.SMEM(decay_rate.shape, jnp.float32),
            pltpu.SMEM(filter_depth.shape, jnp.int32),
            pltpu.SMEM(doc_starts.shape, jnp.int32),
            pltpu.SemaphoreType.DMA((6,)),
            pltpu.SemaphoreType.DMA((count,)),
            pltpu.SemaphoreType.DMA,
            pltpu.SemaphoreType.DMA((count,)),
            pltpu.SemaphoreType.DMA((count,)),
            pltpu.SemaphoreType.DMA((count,)),
            pltpu.SemaphoreType.DMA((count,)),
        ],
        compiler_params=pltpu.CompilerParams(
            collective_id=0, has_side_effects=True, vmem_limit_bytes=VMEM_BYTES
        ),
    )(signal, filter_base, decay_rate, filter_depth, doc_starts)
    unit = jnp.exp2(convolved[tok_rows : tok_rows + 1].astype(jnp.float32)) * (1.0 / TOP)
    mixed = gate_values.astype(jnp.float32) * (
        convolved[:tok_rows].astype(jnp.float32) * unit
        + skip_gain[None, :] * signal.astype(jnp.float32)
    )
    return mixed.astype(jnp.bfloat16)


def body(signal, gate_values, skip_gain, filter_base, decay_rate, filter_depth, doc_starts, count):
    tok_rows, chan_width = signal.shape
    group_count, lag_width = filter_base.shape
    whole_groups = group_count % count == 0 and chan_width % (count * 128) == 0
    fits = tok_rows == 256 and lag_width >= tok_rows * count and count % 4 == 0
    aligned = group_count % 16 == 0
    arrays = (signal, gate_values, skip_gain, filter_base, decay_rate, filter_depth, doc_starts)
    if whole_groups and fits and aligned:
        return exchanged_body(count, *arrays)
    return gathered_body(*arrays)


def solution(mesh):
    in_specs = (
        P("ctx", "chan"),
        P("ctx", "chan"),
        P("chan"),
        P("chan", "ctx"),
        P("chan"),
        P("chan"),
        P(),
    )
    out_specs = P("ctx", "chan")
    return jax.shard_map(
        functools.partial(body, count=mesh.shape["ctx"]),
        mesh=mesh,
        in_specs=in_specs,
        out_specs=out_specs,
        check_vma=False,
    )
```

```python
import functools

import jax
import jax.numpy as jnp
from jax import lax
from jax.experimental import pallas as pl
from jax.experimental.pallas import tpu as pltpu
from jax.sharding import PartitionSpec as P

LAGS = 16384


def begin_rows(doc_starts, positions):
    return jnp.max(
        jnp.where(doc_starts[None, :] <= positions[:, None], doc_starts[None, :], 0), axis=1
    )


def toeplitz_apply(summed, padded, margin, lag_total, out_first, doc_begin, source, anchor):
    out_rows, chan_width = summed.shape
    group_count = padded.shape[0]
    group_size = chan_width // group_count
    source_rows = source.shape[0]
    window_size = out_rows + source_rows - 1
    lowest = out_first - anchor - source_rows + 1
    offset = jnp.clip(lowest, -window_size, lag_total) + margin
    window = lax.dynamic_slice_in_dim(padded, offset, window_size, 1)
    extended = jnp.pad(window, ((0, 0), (0, 1)))
    repeated = jnp.tile(extended, (1, out_rows + 1))
    skewed = repeated[:, : out_rows * (window_size + 2)].reshape(
        group_count, out_rows, window_size + 2
    )
    toeplitz = skewed[:, :, :source_rows][:, :, ::-1]
    doc_mask = (anchor + lax.iota(jnp.int32, source_rows))[None, :] >= doc_begin[:, None]
    toeplitz = jnp.where(doc_mask[None], toeplitz, jnp.zeros((), jnp.bfloat16))
    channels = source.reshape(source_rows, group_count, group_size)
    product = jnp.einsum("gts,sgc->tgc", toeplitz, channels, preferred_element_type=jnp.float32)
    return summed + product.reshape(out_rows, chan_width)


def gathered_body(signal, gate_values, skip_gain, filter_base, decay_rate, filter_depth, doc_starts):
    tok_rows, chan_width = signal.shape
    group_count, lag_width = filter_base.shape
    ctx_index = lax.axis_index("ctx")
    lag_index = ctx_index * lag_width + lax.iota(jnp.int32, lag_width)
    inside = lag_index[None, :] < filter_depth[:, None]
    local_panel = jnp.where(
        inside,
        filter_base.astype(jnp.float32)
        * jnp.exp(-decay_rate[:, None] * lag_index.astype(jnp.float32)[None, :] / LAGS),
        0.0,
    ).astype(jnp.bfloat16)
    filters = lax.all_gather(local_panel, "ctx", axis=1, tiled=True)
    lag_total = filters.shape[1]
    margin = 2 * tok_rows
    padded = jnp.pad(filters, ((0, 0), (margin, margin)))
    first_row = ctx_index * tok_rows
    positions = first_row + lax.iota(jnp.int32, tok_rows)
    doc_begin = begin_rows(doc_starts, positions)

    def add_checked(summed, source, anchor):
        needed = anchor < first_row + tok_rows
        return lax.cond(
            needed,
            lambda carried: toeplitz_apply(
                carried, padded, margin, lag_total, first_row, doc_begin, source, anchor
            ),
            lambda carried: carried,
            summed,
        )

    initial = jnp.zeros((tok_rows, chan_width), jnp.float32)
    summed = initial
    source = lax.all_gather(signal, "ctx", axis=0, tiled=True)
    source_rows = source.shape[0]
    steps_count = source_rows // tok_rows
    stacked = source.reshape(steps_count, tok_rows, chan_width)

    def advance(carried, item):
        one_shard, number = item
        return (add_checked(carried, one_shard, number * tok_rows), None)

    summed, ignored = lax.scan(advance, summed, (stacked, jnp.arange(steps_count, dtype=jnp.int32)))
    mixed = gate_values.astype(jnp.float32) * (
        summed + skip_gain[None, :] * signal.astype(jnp.float32)
    )
    return mixed.astype(jnp.bfloat16)


LINK = jnp.int16
STEPS = 780.0
FLOOR = 30.0
VMEM_BYTES = 60 * 1024 * 1024
MESH = pl.DeviceIdType.MESH


def coded(values):
    size = jnp.maximum(jnp.abs(values), 2.0**-FLOOR)
    steps = jnp.floor((jnp.log2(size) + FLOOR) * STEPS + 0.5)
    return jnp.where(values < 0.0, -steps, steps).astype(jnp.int32).astype(LINK)


def decoded(codes):
    steps = codes.astype(jnp.int32).astype(jnp.float32)
    size = jnp.exp2(jnp.abs(steps) * (1.0 / STEPS) - FLOOR)
    return jnp.where(steps == 0.0, 0.0, jnp.where(steps < 0.0, -size, size))


def exchange_kernel(
    count, masked_blocks, signal_ref, gate_ref, skip_ref, base_ref, decay_ref, depth_ref,
    starts_ref, out_ref, base_buf, taps_all, taps_buf, x_buf, y_buf, y_in, own_signal, gate_buf,
    skip_buf, mixed_buf, strip, decay_mem, depth_mem, starts_mem, local_sems, out_sems, taps_send, taps_recv, send_x, recv_x, send_y, recv_y,
):
    me = lax.axis_index("ctx")
    half = count // 2
    rows = x_buf.shape[0] // count
    width = x_buf.shape[1]
    tap_rows = taps_buf.shape[0]
    groups = tap_rows // count
    window = rows * count

    def lanes(index):
        return pl.ds(pl.multiple_of(index * width, width), width)

    def row_block(index):
        return pl.ds(pl.multiple_of(index * rows, rows), rows)

    barrier = pltpu.get_barrier_semaphore()
    for offset in range(1, count):
        pl.semaphore_signal(
            barrier, inc=1, device_id={"ctx": lax.rem(me + offset, count)}, device_id_type=MESH
        )

    own_x = pltpu.make_async_copy(
        signal_ref.at[:, lanes(me)], x_buf.at[row_block(me)], local_sems.at[0]
    )
    own_x.start()
    starts_copy = pltpu.make_async_copy(starts_ref, starts_mem, local_sems.at[1])
    starts_copy.start()
    base_copy = pltpu.make_async_copy(base_ref.at[:, pl.ds(0, window)], base_buf, local_sems.at[2])
    decay_copy = pltpu.make_async_copy(decay_ref, decay_mem, local_sems.at[3])
    depth_copy = pltpu.make_async_copy(depth_ref, depth_mem, local_sems.at[4])

    @pl.when(me == 0)
    def _():
        base_copy.start()
        decay_copy.start()
        depth_copy.start()

    operand_copies = [
        pltpu.make_async_copy(signal_ref, own_signal, local_sems.at[5]),
        pltpu.make_async_copy(gate_ref, gate_buf, local_sems.at[6]),
        pltpu.make_async_copy(skip_ref, skip_buf, local_sems.at[7]),
    ]
    pl.semaphore_wait(barrier, count - 1)

    def x_copy(peer):
        return pltpu.make_async_remote_copy(
            src_ref=signal_ref.at[:, lanes(peer)],
            dst_ref=x_buf.at[row_block(me)],
            send_sem=send_x.at[peer],
            recv_sem=recv_x.at[me],
            device_id={"ctx": peer},
            device_id_type=MESH,
        )

    def x_arrival(source):
        return pltpu.make_async_remote_copy(
            src_ref=signal_ref.at[:, lanes(source)],
            dst_ref=x_buf.at[row_block(source)],
            send_sem=send_x.at[source],
            recv_sem=recv_x.at[source],
            device_id={"ctx": jnp.int32(source)},
            device_id_type=MESH,
        )

    side = lax.div(me, half)
    place = lax.rem(me, half)
    near = [side * half + lax.rem(place + k, half) for k in range(1, half)]
    far = [(1 - side) * half + lax.rem(place + k, half) for k in range(half)]
    early = place < half // 2

    @pl.when(early)
    def _():
        for peer in far + near:
            x_copy(peer).start()

    @pl.when(jnp.logical_not(early))
    def _():
        for peer in near + far:
            x_copy(peer).start()

    def taps_copy(peer):
        return pltpu.make_async_remote_copy(
            src_ref=taps_all.at[pl.ds(peer * tap_rows, tap_rows)],
            dst_ref=taps_buf,
            send_sem=taps_send.at[peer],
            recv_sem=taps_recv,
            device_id={"ctx": jnp.int32(peer)},
            device_id_type=MESH,
        )

    @pl.when(me == 0)
    def _():
        base_copy.wait()
        decay_copy.wait()
        depth_copy.wait()
        group_rows = groups * count
        group_id = lax.broadcasted_iota(jnp.int32, (group_rows, 128), 0)
        decay = jnp.zeros((group_rows, 128), jnp.float32)
        depth = jnp.zeros((group_rows, 128), jnp.int32)
        for g in range(group_rows):
            decay = jnp.where(group_id == g, decay_mem[g], decay)
            depth = jnp.where(group_id == g, depth_mem[g], depth)
        decay = jnp.concatenate([decay] * (rows // 128), axis=1)
        depth = jnp.concatenate([depth] * (rows // 128), axis=1)
        out_row = lax.broadcasted_iota(jnp.int32, (group_rows * count, group_rows), 0)
        in_row = lax.broadcasted_iota(jnp.int32, (group_rows * count, group_rows), 1)
        placed = jnp.zeros((group_rows * count, rows), jnp.float32)
        for d in range(count):
            lag = d * rows + lax.broadcasted_iota(jnp.int32, (group_rows, rows), 1)
            base = base_buf[:, pl.ds(d * rows, rows)].astype(jnp.float32)
            kept = base * jnp.exp(-decay * lag.astype(jnp.float32) / LAGS)
            panel = jnp.where(lag < depth, kept, 0.0).astype(jnp.bfloat16)
            pick = (out_row == in_row * count + d).astype(jnp.float32).astype(jnp.bfloat16)
            placed += jnp.dot(pick, panel, preferred_element_type=jnp.float32)
        taps_all[...] = placed.astype(jnp.bfloat16)
        for peer in range(1, count):
            taps_copy(peer).start()
        taps_buf[...] = taps_all[pl.ds(0, tap_rows), :]

    for copy in operand_copies:
        copy.start()

    @pl.when(me != 0)
    def _():
        taps_copy(1).wait_recv()

    row_id = lax.broadcasted_iota(jnp.int32, (rows, rows), 0)
    col_id = lax.broadcasted_iota(jnp.int32, (rows, rows), 1)
    flip = (row_id + col_id == rows - 1).astype(jnp.float32).astype(jnp.bfloat16)
    flipped = jnp.dot(taps_buf[...], flip, preferred_element_type=jnp.float32)
    span = window + rows
    step = 32
    for g in range(groups):
        pieces = [
            flipped[g * count + d : g * count + d + 1, :] for d in range(count - 1, -1, -1)
        ]
        line = jnp.concatenate(pieces + [jnp.zeros((1, rows), jnp.float32)], axis=1)
        spread = jnp.broadcast_to(line, (step, span))
        for base in range(0, rows, step):
            turned = pltpu.roll(
                spread, (span - (rows - 1) + base) % span, 1, stride=1, stride_axis=0
            )
            strip[g, pl.ds(base, step), :] = turned[:, :window].astype(jnp.bfloat16)

    starts_copy.wait()
    own_x.wait()
    docs = starts_mem.shape[0]
    head_rows = masked_blocks * rows
    lane_group = lax.broadcasted_iota(jnp.int32, (rows, width), 1) // (width // groups)

    def wait_for(block):
        @pl.when(me != block)
        def _():
            x_arrival(block).wait_recv()

    def y_copy(block):
        return pltpu.make_async_remote_copy(
            src_ref=y_buf.at[row_block(block)],
            dst_ref=y_in.at[row_block(me)],
            send_sem=send_y.at[block],
            recv_sem=recv_y.at[me],
            device_id={"ctx": jnp.int32(block)},
            device_id_type=MESH,
        )

    def y_arrival(source):
        return pltpu.make_async_remote_copy(
            src_ref=y_buf.at[row_block(source)],
            dst_ref=y_in.at[row_block(source)],
            send_sem=send_y.at[source],
            recv_sem=recv_y.at[source],
            device_id={"ctx": jnp.int32(source)},
            device_id_type=MESH,
        )

    def send_back(block, total):
        y_buf[pl.ds(block * rows, rows), :] = coded(total)

        @pl.when(me != block)
        def _():
            y_copy(block).start()

    for block in range(masked_blocks):
        wait_for(block)
        depth = (block + 1) * rows
        t_id = block * rows + lax.broadcasted_iota(jnp.int32, (rows, depth), 0)
        s_id = lax.broadcasted_iota(jnp.int32, (rows, depth), 1)
        begin = jnp.zeros((rows, depth), jnp.int32)
        for k in range(docs):
            start = starts_mem[k]
            begin = jnp.where(start <= t_id, jnp.maximum(begin, start), begin)
        seen = s_id >= begin
        total = jnp.zeros((rows, width), jnp.float32)
        for g in range(groups):
            taps = jnp.where(
                seen, strip[g, :, pl.ds(window - depth, depth)].astype(jnp.float32), 0.0
            ).astype(jnp.bfloat16)
            part = jnp.dot(taps, x_buf[pl.ds(0, depth), :], preferred_element_type=jnp.float32)
            total = jnp.where(lane_group == g, part, total)
        send_back(block, total)

    head_id = lax.broadcasted_iota(jnp.int32, (head_rows, width), 0)
    x_head = x_buf[pl.ds(0, head_rows), :].astype(jnp.float32)
    x_buf[pl.ds(0, head_rows), :] = jnp.where(
        head_id >= starts_mem[docs - 1], x_head, 0.0
    ).astype(jnp.bfloat16)
    for block in range(masked_blocks, count):
        wait_for(block)
        depth = (block + 1) * rows
        total = jnp.zeros((rows, width), jnp.float32)
        for g in range(groups):
            part = jnp.dot(
                strip[g, :, pl.ds(window - depth, depth)],
                x_buf[pl.ds(0, depth), :],
                preferred_element_type=jnp.float32,
            )
            total = jnp.where(lane_group == g, part, total)
        send_back(block, total)

    for copy in operand_copies:
        copy.wait()

    def out_copy(index):
        return pltpu.make_async_copy(
            mixed_buf.at[:, lanes(index)], out_ref.at[:, lanes(index)], out_sems.at[index]
        )

    def mix(index, codes):
        direct = skip_buf[:, lanes(index)] * own_signal[:, lanes(index)].astype(jnp.float32)
        gates = gate_buf[:, lanes(index)].astype(jnp.float32)
        mixed_buf[:, lanes(index)] = (gates * (decoded(codes) + direct)).astype(jnp.bfloat16)
        out_copy(index).start()

    mix(me, y_buf[row_block(me), :])
    for peer in near + far:
        y_arrival(peer).wait_recv()
        mix(peer, y_in[row_block(peer), :])

    @pl.when(me == 0)
    def _():
        for peer in range(1, count):
            taps_copy(peer).wait_send()

    for peer in near + far:
        x_copy(peer).wait_send()
    for peer in near + far:
        y_arrival(peer).wait_send()
    for index in range(count):
        out_copy(index).wait()


def exchanged_body(
    count, signal, gate_values, skip_gain, filter_base, decay_rate, filter_depth, doc_starts
):
    tok_rows, chan_width = signal.shape
    group_count, lag_width = filter_base.shape
    window = tok_rows * count
    width = chan_width // count
    tap_rows = group_count
    groups = group_count // count
    masked_blocks = max(1, count // 4)
    return pl.pallas_call(
        functools.partial(exchange_kernel, count, masked_blocks),
        out_shape=jax.ShapeDtypeStruct((tok_rows, chan_width), jnp.bfloat16),
        in_specs=[
            pl.BlockSpec(memory_space=pl.ANY),
        ]
        * 7,
        out_specs=pl.BlockSpec(memory_space=pl.ANY),
        scratch_shapes=[
            pltpu.VMEM((group_count, window), jnp.bfloat16),
            pltpu.VMEM((tap_rows * count, tok_rows), jnp.bfloat16),
            pltpu.VMEM((tap_rows, tok_rows), jnp.bfloat16),
            pltpu.VMEM((window, width), jnp.bfloat16),
            pltpu.VMEM((window, width), LINK),
            pltpu.VMEM((window, width), LINK),
            pltpu.VMEM((tok_rows, chan_width), jnp.bfloat16),
            pltpu.VMEM((tok_rows, chan_width), jnp.bfloat16),
            pltpu.VMEM((1, chan_width), jnp.float32),
            pltpu.VMEM((tok_rows, chan_width), jnp.bfloat16),
            pltpu.VMEM((groups, tok_rows, window), jnp.bfloat16),
            pltpu.SMEM(decay_rate.shape, jnp.float32),
            pltpu.SMEM(filter_depth.shape, jnp.int32),
            pltpu.SMEM(doc_starts.shape, jnp.int32),
            pltpu.SemaphoreType.DMA((8,)),
            pltpu.SemaphoreType.DMA((count,)),
            pltpu.SemaphoreType.DMA((count,)),
            pltpu.SemaphoreType.DMA,
            pltpu.SemaphoreType.DMA((count,)),
            pltpu.SemaphoreType.DMA((count,)),
            pltpu.SemaphoreType.DMA((count,)),
            pltpu.SemaphoreType.DMA((count,)),
        ],
        compiler_params=pltpu.CompilerParams(
            collective_id=0, has_side_effects=True, vmem_limit_bytes=VMEM_BYTES
        ),
    )(
        signal,
        gate_values,
        skip_gain.reshape(1, chan_width),
        filter_base,
        decay_rate,
        filter_depth,
        doc_starts,
    )


def body(signal, gate_values, skip_gain, filter_base, decay_rate, filter_depth, doc_starts, count):
    tok_rows, chan_width = signal.shape
    group_count, lag_width = filter_base.shape
    whole_groups = group_count % count == 0 and chan_width % (count * 128) == 0
    fits = tok_rows == 256 and lag_width >= tok_rows * count and count % 4 == 0
    aligned = group_count % 16 == 0
    arrays = (signal, gate_values, skip_gain, filter_base, decay_rate, filter_depth, doc_starts)
    if whole_groups and fits and aligned:
        return exchanged_body(count, *arrays)
    return gathered_body(*arrays)


def solution(mesh):
    in_specs = (
        P("ctx", "chan"),
        P("ctx", "chan"),
        P("chan"),
        P("chan", "ctx"),
        P("chan"),
        P("chan"),
        P(),
    )
    out_specs = P("ctx", "chan")
    return jax.shard_map(
        functools.partial(body, count=mesh.shape["ctx"]),
        mesh=mesh,
        in_specs=in_specs,
        out_specs=out_specs,
        check_vma=False,
    )
```

```python
import functools

import jax
import jax.numpy as jnp
from jax import lax
from jax.experimental import pallas as pl
from jax.experimental.pallas import tpu as pltpu
from jax.sharding import PartitionSpec as P

LAGS = 16384


def begin_rows(doc_starts, positions):
    return jnp.max(
        jnp.where(doc_starts[None, :] <= positions[:, None], doc_starts[None, :], 0), axis=1
    )


def toeplitz_apply(summed, padded, margin, lag_total, out_first, doc_begin, source, anchor):
    out_rows, chan_width = summed.shape
    group_count = padded.shape[0]
    group_size = chan_width // group_count
    source_rows = source.shape[0]
    window_size = out_rows + source_rows - 1
    lowest = out_first - anchor - source_rows + 1
    offset = jnp.clip(lowest, -window_size, lag_total) + margin
    window = lax.dynamic_slice_in_dim(padded, offset, window_size, 1)
    extended = jnp.pad(window, ((0, 0), (0, 1)))
    repeated = jnp.tile(extended, (1, out_rows + 1))
    skewed = repeated[:, : out_rows * (window_size + 2)].reshape(
        group_count, out_rows, window_size + 2
    )
    toeplitz = skewed[:, :, :source_rows][:, :, ::-1]
    doc_mask = (anchor + lax.iota(jnp.int32, source_rows))[None, :] >= doc_begin[:, None]
    toeplitz = jnp.where(doc_mask[None], toeplitz, jnp.zeros((), jnp.bfloat16))
    channels = source.reshape(source_rows, group_count, group_size)
    product = jnp.einsum("gts,sgc->tgc", toeplitz, channels, preferred_element_type=jnp.float32)
    return summed + product.reshape(out_rows, chan_width)


def gathered_body(signal, gate_values, skip_gain, filter_base, decay_rate, filter_depth, doc_starts):
    tok_rows, chan_width = signal.shape
    group_count, lag_width = filter_base.shape
    ctx_index = lax.axis_index("ctx")
    lag_index = ctx_index * lag_width + lax.iota(jnp.int32, lag_width)
    inside = lag_index[None, :] < filter_depth[:, None]
    local_panel = jnp.where(
        inside,
        filter_base.astype(jnp.float32)
        * jnp.exp(-decay_rate[:, None] * lag_index.astype(jnp.float32)[None, :] / LAGS),
        0.0,
    ).astype(jnp.bfloat16)
    filters = lax.all_gather(local_panel, "ctx", axis=1, tiled=True)
    lag_total = filters.shape[1]
    margin = 2 * tok_rows
    padded = jnp.pad(filters, ((0, 0), (margin, margin)))
    first_row = ctx_index * tok_rows
    positions = first_row + lax.iota(jnp.int32, tok_rows)
    doc_begin = begin_rows(doc_starts, positions)

    def add_checked(summed, source, anchor):
        needed = anchor < first_row + tok_rows
        return lax.cond(
            needed,
            lambda carried: toeplitz_apply(
                carried, padded, margin, lag_total, first_row, doc_begin, source, anchor
            ),
            lambda carried: carried,
            summed,
        )

    initial = jnp.zeros((tok_rows, chan_width), jnp.float32)
    summed = initial
    source = lax.all_gather(signal, "ctx", axis=0, tiled=True)
    source_rows = source.shape[0]
    steps_count = source_rows // tok_rows
    stacked = source.reshape(steps_count, tok_rows, chan_width)

    def advance(carried, item):
        one_shard, number = item
        return (add_checked(carried, one_shard, number * tok_rows), None)

    summed, ignored = lax.scan(advance, summed, (stacked, jnp.arange(steps_count, dtype=jnp.int32)))
    mixed = gate_values.astype(jnp.float32) * (
        summed + skip_gain[None, :] * signal.astype(jnp.float32)
    )
    return mixed.astype(jnp.bfloat16)


LINK = jnp.int16
STEPS = 780.0
FLOOR = 30.0
VMEM_BYTES = 60 * 1024 * 1024
MESH = pl.DeviceIdType.MESH


def coded(values):
    size = jnp.maximum(jnp.abs(values), 2.0**-FLOOR)
    steps = jnp.floor((jnp.log2(size) + FLOOR) * STEPS + 0.5)
    return jnp.where(values < 0.0, -steps, steps).astype(jnp.int32).astype(LINK)


def decoded(codes):
    steps = codes.astype(jnp.int32).astype(jnp.float32)
    size = jnp.exp2(jnp.abs(steps) * (1.0 / STEPS) - FLOOR)
    return jnp.where(steps == 0.0, 0.0, jnp.where(steps < 0.0, -size, size))


def exchange_kernel(
    count, masked_blocks, signal_ref, gate_ref, skip_ref, base_ref, decay_ref, depth_ref,
    starts_ref, out_ref, base_buf, taps_all, taps_buf, x_buf, y_buf, y_in, own_signal, gate_buf,
    skip_buf, mixed_buf, strip, decay_mem, depth_mem, starts_mem, local_sems, out_sems, taps_send, taps_recv, send_x, recv_x, send_y, recv_y,
):
    me = lax.axis_index("ctx")
    half = count // 2
    rows = x_buf.shape[0] // count
    width = x_buf.shape[1]
    tap_rows = taps_buf.shape[0]
    groups = tap_rows // count
    window = rows * count

    def lanes(index):
        return pl.ds(pl.multiple_of(index * width, width), width)

    def row_block(index):
        return pl.ds(pl.multiple_of(index * rows, rows), rows)

    barrier = pltpu.get_barrier_semaphore()
    for offset in range(1, count):
        pl.semaphore_signal(
            barrier, inc=1, device_id={"ctx": lax.rem(me + offset, count)}, device_id_type=MESH
        )

    own_x = pltpu.make_async_copy(
        signal_ref.at[:, lanes(me)], x_buf.at[row_block(me)], local_sems.at[0]
    )
    own_x.start()
    starts_copy = pltpu.make_async_copy(starts_ref, starts_mem, local_sems.at[1])
    starts_copy.start()
    base_copy = pltpu.make_async_copy(base_ref.at[:, pl.ds(0, window)], base_buf, local_sems.at[2])
    decay_copy = pltpu.make_async_copy(decay_ref, decay_mem, local_sems.at[3])
    depth_copy = pltpu.make_async_copy(depth_ref, depth_mem, local_sems.at[4])

    @pl.when(me == 0)
    def _():
        base_copy.start()
        decay_copy.start()
        depth_copy.start()

    operand_copies = [
        pltpu.make_async_copy(signal_ref, own_signal, local_sems.at[5]),
        pltpu.make_async_copy(gate_ref, gate_buf, local_sems.at[6]),
        pltpu.make_async_copy(skip_ref, skip_buf, local_sems.at[7]),
    ]
    pl.semaphore_wait(barrier, count - 1)

    def x_copy(peer):
        return pltpu.make_async_remote_copy(
            src_ref=signal_ref.at[:, lanes(peer)],
            dst_ref=x_buf.at[row_block(me)],
            send_sem=send_x.at[peer],
            recv_sem=recv_x.at[me],
            device_id={"ctx": peer},
            device_id_type=MESH,
        )

    def x_arrival(source):
        return pltpu.make_async_remote_copy(
            src_ref=signal_ref.at[:, lanes(source)],
            dst_ref=x_buf.at[row_block(source)],
            send_sem=send_x.at[source],
            recv_sem=recv_x.at[source],
            device_id={"ctx": jnp.int32(source)},
            device_id_type=MESH,
        )

    side = lax.div(me, half)
    place = lax.rem(me, half)
    near = [side * half + lax.rem(place + k, half) for k in range(1, half)]
    far = [(1 - side) * half + lax.rem(place + k, half) for k in range(half)]
    early = place < half // 2

    @pl.when(early)
    def _():
        for peer in far + near:
            x_copy(peer).start()

    @pl.when(jnp.logical_not(early))
    def _():
        for peer in near + far:
            x_copy(peer).start()

    def taps_copy(peer):
        return pltpu.make_async_remote_copy(
            src_ref=taps_all.at[pl.ds(peer * tap_rows, tap_rows)],
            dst_ref=taps_buf,
            send_sem=taps_send.at[peer],
            recv_sem=taps_recv,
            device_id={"ctx": jnp.int32(peer)},
            device_id_type=MESH,
        )

    @pl.when(me == 0)
    def _():
        base_copy.wait()
        decay_copy.wait()
        depth_copy.wait()
        group_rows = groups * count
        group_id = lax.broadcasted_iota(jnp.int32, (group_rows, 128), 0)
        decay = jnp.zeros((group_rows, 128), jnp.float32)
        depth = jnp.zeros((group_rows, 128), jnp.int32)
        for g in range(group_rows):
            decay = jnp.where(group_id == g, decay_mem[g], decay)
            depth = jnp.where(group_id == g, depth_mem[g], depth)
        decay = jnp.concatenate([decay] * (rows // 128), axis=1)
        depth = jnp.concatenate([depth] * (rows // 128), axis=1)
        out_row = lax.broadcasted_iota(jnp.int32, (group_rows * count, group_rows), 0)
        in_row = lax.broadcasted_iota(jnp.int32, (group_rows * count, group_rows), 1)
        placed = jnp.zeros((group_rows * count, rows), jnp.float32)
        for d in range(count):
            lag = d * rows + lax.broadcasted_iota(jnp.int32, (group_rows, rows), 1)
            base = base_buf[:, pl.ds(d * rows, rows)].astype(jnp.float32)
            kept = base * jnp.exp(-decay * lag.astype(jnp.float32) / LAGS)
            panel = jnp.where(lag < depth, kept, 0.0).astype(jnp.bfloat16)
            pick = (out_row == in_row * count + d).astype(jnp.float32).astype(jnp.bfloat16)
            placed += jnp.dot(pick, panel, preferred_element_type=jnp.float32)
        taps_all[...] = placed.astype(jnp.bfloat16)
        for peer in range(1, count):
            taps_copy(peer).start()
        taps_buf[...] = taps_all[pl.ds(0, tap_rows), :]

    for copy in operand_copies:
        copy.start()

    @pl.when(me != 0)
    def _():
        taps_copy(1).wait_recv()

    row_id = lax.broadcasted_iota(jnp.int32, (rows, rows), 0)
    col_id = lax.broadcasted_iota(jnp.int32, (rows, rows), 1)
    flip = (row_id + col_id == rows - 1).astype(jnp.float32).astype(jnp.bfloat16)
    flipped = jnp.dot(taps_buf[...], flip, preferred_element_type=jnp.float32)
    span = window + rows
    step = 32
    for g in range(groups):
        pieces = [
            flipped[g * count + d : g * count + d + 1, :] for d in range(count - 1, -1, -1)
        ]
        line = jnp.concatenate(pieces + [jnp.zeros((1, rows), jnp.float32)], axis=1)
        spread = jnp.broadcast_to(line, (step, span))
        for base in range(0, rows, step):
            turned = pltpu.roll(
                spread, (span - (rows - 1) + base) % span, 1, stride=1, stride_axis=0
            )
            strip[g, pl.ds(base, step), :] = turned[:, :window].astype(jnp.bfloat16)

    starts_copy.wait()
    own_x.wait()
    docs = starts_mem.shape[0]
    head_rows = masked_blocks * rows
    lane_group = lax.broadcasted_iota(jnp.int32, (rows, width), 1) // (width // groups)

    def wait_for(block):
        @pl.when(me != block)
        def _():
            x_arrival(block).wait_recv()

    def y_copy(block):
        return pltpu.make_async_remote_copy(
            src_ref=y_buf.at[row_block(block)],
            dst_ref=y_in.at[row_block(me)],
            send_sem=send_y.at[block],
            recv_sem=recv_y.at[me],
            device_id={"ctx": jnp.int32(block)},
            device_id_type=MESH,
        )

    def y_arrival(source):
        return pltpu.make_async_remote_copy(
            src_ref=y_buf.at[row_block(source)],
            dst_ref=y_in.at[row_block(source)],
            send_sem=send_y.at[source],
            recv_sem=recv_y.at[source],
            device_id={"ctx": jnp.int32(source)},
            device_id_type=MESH,
        )

    def send_back(block, total):
        y_buf[pl.ds(block * rows, rows), :] = coded(total)

        @pl.when(me != block)
        def _():
            y_copy(block).start()

    for block in range(masked_blocks):
        wait_for(block)
        depth = (block + 1) * rows
        t_id = block * rows + lax.broadcasted_iota(jnp.int32, (rows, depth), 0)
        s_id = lax.broadcasted_iota(jnp.int32, (rows, depth), 1)
        begin = jnp.zeros((rows, depth), jnp.int32)
        for k in range(docs):
            start = starts_mem[k]
            begin = jnp.where(start <= t_id, jnp.maximum(begin, start), begin)
        seen = s_id >= begin
        total = jnp.zeros((rows, width), jnp.float32)
        for g in range(groups):
            taps = jnp.where(
                seen, strip[g, :, pl.ds(window - depth, depth)].astype(jnp.float32), 0.0
            ).astype(jnp.bfloat16)
            part = jnp.dot(taps, x_buf[pl.ds(0, depth), :], preferred_element_type=jnp.float32)
            total = jnp.where(lane_group == g, part, total)
        send_back(block, total)

    head_id = lax.broadcasted_iota(jnp.int32, (head_rows, width), 0)
    x_head = x_buf[pl.ds(0, head_rows), :].astype(jnp.float32)
    x_buf[pl.ds(0, head_rows), :] = jnp.where(
        head_id >= starts_mem[docs - 1], x_head, 0.0
    ).astype(jnp.bfloat16)
    for block in range(masked_blocks, count):
        wait_for(block)
        depth = (block + 1) * rows
        total = jnp.zeros((rows, width), jnp.float32)
        for g in range(groups):
            part = jnp.dot(
                strip[g, :, pl.ds(window - depth, depth)],
                x_buf[pl.ds(0, depth), :],
                preferred_element_type=jnp.float32,
            )
            total = jnp.where(lane_group == g, part, total)
        send_back(block, total)

    for copy in operand_copies:
        copy.wait()

    def out_copy(index):
        return pltpu.make_async_copy(
            mixed_buf.at[:, lanes(index)], out_ref.at[:, lanes(index)], out_sems.at[index]
        )

    def mix(index, codes):
        direct = skip_buf[:, lanes(index)] * own_signal[:, lanes(index)].astype(jnp.float32)
        gates = gate_buf[:, lanes(index)].astype(jnp.float32)
        mixed_buf[:, lanes(index)] = (gates * (decoded(codes) + direct)).astype(jnp.bfloat16)
        out_copy(index).start()

    mix(me, y_buf[row_block(me), :])
    for peer in near + far:
        y_arrival(peer).wait_recv()
        mix(peer, y_in[row_block(peer), :])

    @pl.when(me == 0)
    def _():
        for peer in range(1, count):
            taps_copy(peer).wait_send()

    for peer in near + far:
        x_copy(peer).wait_send()
    for peer in near + far:
        y_arrival(peer).wait_send()
    for index in range(count):
        out_copy(index).wait()


def exchanged_body(
    count, signal, gate_values, skip_gain, filter_base, decay_rate, filter_depth, doc_starts
):
    tok_rows, chan_width = signal.shape
    group_count, lag_width = filter_base.shape
    window = tok_rows * count
    width = chan_width // count
    tap_rows = group_count
    groups = group_count // count
    masked_blocks = max(1, count // 4)
    return pl.pallas_call(
        functools.partial(exchange_kernel, count, masked_blocks),
        out_shape=pltpu.VMEM((tok_rows, chan_width), jnp.bfloat16),
        in_specs=[
            pl.BlockSpec(memory_space=pl.ANY),
        ]
        * 7,
        out_specs=pl.BlockSpec(memory_space=pl.ANY),
        scratch_shapes=[
            pltpu.VMEM((group_count, window), jnp.bfloat16),
            pltpu.VMEM((tap_rows * count, tok_rows), jnp.bfloat16),
            pltpu.VMEM((tap_rows, tok_rows), jnp.bfloat16),
            pltpu.VMEM((window, width), jnp.bfloat16),
            pltpu.VMEM((window, width), LINK),
            pltpu.VMEM((window, width), LINK),
            pltpu.VMEM((tok_rows, chan_width), jnp.bfloat16),
            pltpu.VMEM((tok_rows, chan_width), jnp.bfloat16),
            pltpu.VMEM((1, chan_width), jnp.float32),
            pltpu.VMEM((tok_rows, chan_width), jnp.bfloat16),
            pltpu.VMEM((groups, tok_rows, window), jnp.bfloat16),
            pltpu.SMEM(decay_rate.shape, jnp.float32),
            pltpu.SMEM(filter_depth.shape, jnp.int32),
            pltpu.SMEM(doc_starts.shape, jnp.int32),
            pltpu.SemaphoreType.DMA((8,)),
            pltpu.SemaphoreType.DMA((count,)),
            pltpu.SemaphoreType.DMA((count,)),
            pltpu.SemaphoreType.DMA,
            pltpu.SemaphoreType.DMA((count,)),
            pltpu.SemaphoreType.DMA((count,)),
            pltpu.SemaphoreType.DMA((count,)),
            pltpu.SemaphoreType.DMA((count,)),
        ],
        compiler_params=pltpu.CompilerParams(
            collective_id=0, has_side_effects=True, vmem_limit_bytes=VMEM_BYTES
        ),
    )(
        signal,
        gate_values,
        skip_gain.reshape(1, chan_width),
        filter_base,
        decay_rate,
        filter_depth,
        doc_starts,
    )


def body(signal, gate_values, skip_gain, filter_base, decay_rate, filter_depth, doc_starts, count):
    tok_rows, chan_width = signal.shape
    group_count, lag_width = filter_base.shape
    whole_groups = group_count % count == 0 and chan_width % (count * 128) == 0
    fits = tok_rows == 256 and lag_width >= tok_rows * count and count % 4 == 0
    aligned = group_count % 16 == 0
    arrays = (signal, gate_values, skip_gain, filter_base, decay_rate, filter_depth, doc_starts)
    if whole_groups and fits and aligned:
        return exchanged_body(count, *arrays)
    return gathered_body(*arrays)


def solution(mesh):
    in_specs = (
        P("ctx", "chan"),
        P("ctx", "chan"),
        P("chan"),
        P("chan", "ctx"),
        P("chan"),
        P("chan"),
        P(),
    )
    out_specs = P("ctx", "chan")
    return jax.shard_map(
        functools.partial(body, count=mesh.shape["ctx"]),
        mesh=mesh,
        in_specs=in_specs,
        out_specs=out_specs,
        check_vma=False,
    )
```
